256 devices in a mesh: grp: 8 (over y, z_hi), ep: 32 (over x, z_lo, core).
Axes of the slice: x: 4, y: 4, z: 8 (z_hi: 2, z_lo: 4; z = z_hi * 4 + z_lo), core: 2. Of those that a mesh axis runs over, the one named last changes fastest.
Arguments:
- tokens: bfloat16 [4096, 5120], P('ep', 'grp'), may hold values from -6 to 6
- out_grad: bfloat16 [4096, 5120], P('ep', 'grp'), may hold values from -1.5 to 1.5
- expert_ids: int32 [4096, 6], P('ep'), may hold values from 0 to 23, all different within a row; in each aligned block of 128 rows (0 to 127, 128 to 255, ...) at most 40 rows name the same one
- route_probs: bfloat16 [4096, 6], P('ep'), may hold values from 0.049804688 to 0.59765625
- slot_expert: int32 [32], replicated, may hold values from 0 to 23, as said below
- w_gate: bfloat16 [32, 5120, 1024], P('ep', 'grp'), as said below
- w_up: bfloat16 [32, 5120, 1024], P('ep', 'grp'), as said below
- w_down: bfloat16 [32, 5120, 1024], P('ep', 'grp'), as said below
Outputs:
- in_grad: bfloat16 [4096, 5120], P('ep', 'grp')
- grad_gate: bfloat16 [32, 5120, 1024], P('ep', 'grp')
- grad_up: bfloat16 [32, 5120, 1024], P('ep', 'grp')
- grad_down: bfloat16 [32, 5120, 1024], P('ep', 'grp')
The draws below stay inside these ranges and needn't reach their ends.
Inputs may be any that keep to these rules, and one draw needn't show every extreme that they name: `expert_ids`: in the rows of one index of ep, no expert is named by more than 40 tokens; some expert is named by exactly 40 in some block. `slot_expert`: every expert 0 to 23 is held by at least one of the 32 slots. `w_gate`: slots that hold the same expert hold equal weights. `w_up`: slots that hold the same expert hold equal weights. `w_down`: slots that hold the same expert hold equal weights.
All inputs are finite; a program needn't handle non-finite values.
Results may differ from the reference program's by a relative error of at most 0.03.
Values may be sent and summed in bfloat16 or wider, within the bound.
No kernel may reach another device: no remote copies, remote signals or barrier semaphores. Data moves between devices by JAX's collectives and lax.ppermute only.
A program may use at most 128 MiB of HBM per device.

```python
import math
import jax
import jax.numpy as jnp
import numpy as np
from jax import lax

D = 5120
TOPK = 6
H = 1024
TOK_DEV = 128
TOKENS = 4096
FLIGHT = 24
CAP = 40
N_GRP = 8
N_EP = 32


def placement(key):
    base = jax.random.permutation(jax.random.fold_in(key, 11), FLIGHT).astype(jnp.int32)
    spare = N_EP - FLIGHT
    first = jax.random.randint(jax.random.fold_in(key, 12), (spare,), 0, FLIGHT)
    second = jax.random.randint(jax.random.fold_in(key, 13), (spare,), 0, FLIGHT)
    hottest = jnp.minimum(first, second)
    layout = jnp.concatenate([base, base[hottest]])
    order = jax.random.permutation(jax.random.fold_in(key, 14), N_EP)
    return layout[order].astype(jnp.int32)


def expert_tables(key, salt, factor):
    base = jax.random.normal(jax.random.fold_in(key, salt), (FLIGHT, D, H), jnp.float32) * factor
    return jnp.take(base, placement(key), axis=0).astype(jnp.bfloat16)


def draw_slot_expert(key, part):
    return placement(key)


def draw_w_gate(key, part):
    return expert_tables(key, 21, D ** (-0.5))


def draw_w_up(key, part):
    return expert_tables(key, 22, D ** (-0.5))


def draw_w_down(key, part):
    return expert_tables(key, 23, H ** (-0.5))


def block_levels(stream_key, extent, pieces, low, high):
    level, own = 1.0, jax.random.fold_in(stream_key, 6)
    for axis_at, shards_of in pieces:
        steps = jnp.exp(jax.random.uniform(jax.random.fold_in(own, axis_at), (shards_of,), jnp.float32, low / len(pieces), high / len(pieces)))
        level = level * jnp.repeat(steps, extent[axis_at] // shards_of).reshape([-1 if axis == axis_at else 1 for axis in range(len(extent))])
    return level


def shared_out(key, own, number, rows, count, top, most, skew):
    order = jax.random.permutation(key, count)
    heavy_load, ordinary = shares(count, rows * top, most, skew, True), shares(count, rows * top, most, skew, False)
    places = jnp.arange(count)

    def named(lengths, rotation):
        used = int((lengths > 0).sum())
        fixed = max(1, used // 4)
        passed = fixed + (places - fixed + rotation * (used - fixed)) % max(1, count - fixed)
        return jnp.zeros((count,), jnp.int32).at[order[jnp.where(places < fixed, places, passed)]].set(jnp.asarray(lengths, jnp.int32))

    lengths = jnp.where(number % 4 == 0, named(heavy_load, number // 4), named(ordinary, number - number // 4 - 1))
    mixed = jax.random.permutation(jax.random.fold_in(own, 3), count)
    source_of, sink = mixed[0:count // 2 * 2:2], mixed[1:count // 2 * 2:2]
    margin = jnp.minimum(lengths[source_of] - 1, most - lengths[sink]) // 2
    margin = jnp.where((source_of == order[0]) | (sink == order[0]) | (lengths[sink] == 0), 0, jnp.maximum(margin, 0))
    passed = jax.random.randint(jax.random.fold_in(own, 4), (count // 2,), 0, 1 << 20) % (margin + 1)
    lengths = lengths.at[source_of].add(-passed).at[sink].add(passed)
    members = jnp.searchsorted(jnp.cumsum(lengths), jnp.arange(rows * top), side="right").astype(jnp.int32)
    listing = members.reshape(top, rows).T
    listing = listing[jax.random.permutation(jax.random.fold_in(own, 1), rows)]
    rotation = jax.random.randint(jax.random.fold_in(own, 2), (rows, 1), 0, top)
    return jnp.take_along_axis(listing, (jnp.arange(top)[None, :] + rotation) % top, axis=1)


def shares(count, total, most, slope, full):
    loads = [(1 << 20) // math.isqrt(rank ** slope) + 1 for rank in range(1, count + 1)]
    largest = most if full else min(most, max(-(-total // count), total * loads[0] // sum(loads)))
    least = 1 if total - largest >= count - 1 else 0
    holding, spare = [largest] + [least] * (count - 1), total - largest - least * (count - 1)
    while spare > 0:
        candidates = [i for i in range(1, count) if holding[i] < largest] or [i for i in range(1, count) if holding[i] < most]
        mass, remaining = sum([loads[i] for i in candidates]), spare
        for i in candidates:
            more = min(most - holding[i], max(1, remaining * loads[i] // mass), spare)
            holding[i] = holding[i] + more
            spare = spare - more
    return np.array(holding)


def bell_draw(stream_key, dims, scale, most, split=(), held_as=jnp.bfloat16):
    array = scale * jax.random.normal(stream_key, dims, jnp.float32)
    if split:
        array = array * block_levels(stream_key, dims, split, -0.22, 0.18)
    return jnp.clip(array, -most, most).astype(held_as)


def setup_inputs(seed: int = 0) -> dict:
    streams_of = jax.random.split(jax.random.key(seed), 9)
    tokens = bell_draw(streams_of[0], (TOKENS, D), 1.0, 6.0, ((0, 32), (1, 8)))
    out_grad = bell_draw(streams_of[1], (TOKENS, D), 0.25, 1.5, ((0, 32), (1, 8)))
    expert_ids_keys = jax.random.split(jax.random.fold_in(streams_of[2], 1), TOKENS // TOK_DEV)
    expert_ids_turns = jax.random.permutation(jax.random.fold_in(streams_of[2], 3), TOKENS // TOK_DEV)
    expert_ids = jax.vmap(lambda own, number: shared_out(jax.random.fold_in(streams_of[2], 2), own, number, TOK_DEV, FLIGHT, TOPK, CAP, 2))(expert_ids_keys, expert_ids_turns).reshape((TOKENS, TOPK))
    route_probs = jnp.clip(0.049804688 + 0.54785156 * jax.random.uniform(streams_of[3], (TOKENS, TOPK), jnp.float32) ** block_levels(streams_of[3], (TOKENS, TOPK), ((0, 32),), -0.2, 0.2), 0.049804688, 0.59765625).astype(jnp.bfloat16)
    slot_expert = draw_slot_expert(jax.random.fold_in(streams_of[8], 71), 0)
    w_gate = draw_w_gate(jax.random.fold_in(streams_of[8], 71), 0)
    w_up = draw_w_up(jax.random.fold_in(streams_of[8], 71), 0)
    w_down = draw_w_down(jax.random.fold_in(streams_of[8], 71), 0)
    return {"tokens": tokens, "out_grad": out_grad, "expert_ids": expert_ids, "route_probs": route_probs, "slot_expert": slot_expert, "w_gate": w_gate, "w_up": w_up, "w_down": w_down}


def activate(gate, up_sum, grad_hidden):
    sigma = jax.nn.sigmoid(gate)
    swish = gate * sigma
    hidden = (swish * up_sum).astype(jnp.bfloat16)
    grad_up = (grad_hidden * swish).astype(jnp.bfloat16)
    grad_gate = (grad_hidden * up_sum * sigma * (1.0 + gate * (1.0 - sigma))).astype(jnp.bfloat16)
    return hidden, grad_gate, grad_up


def split_sum(rows, weight):
    count = rows.shape[0]
    left = rows.reshape(count, N_GRP, D // N_GRP).astype(jnp.float32)
    right = weight.reshape(N_GRP, D // N_GRP, H).astype(jnp.float32)
    parts = jnp.einsum("rgd,gdh->grh", left, right).astype(jnp.bfloat16)
    return jnp.sum(parts.astype(jnp.float32), axis=0)


def reference(tokens, out_grad, expert_ids, route_probs, slot_expert, w_gate, w_up, w_down):
    rows_total = TOKENS * TOPK
    slot_ids = jnp.arange(N_EP, dtype=jnp.int32)
    same_expert = (slot_expert[:, None] == slot_expert[None, :]).astype(jnp.int32)
    earlier = (slot_ids[:, None] > slot_ids[None, :]).astype(jnp.int32)
    replica_rank = jnp.sum(same_expert * earlier, axis=1)
    flat_ids = expert_ids.reshape(-1)
    source = (jnp.arange(rows_total, dtype=jnp.int32) // (TOK_DEV * TOPK)).astype(jnp.int32)
    hosting = flat_ids[:, None] == slot_expert[None, :]
    replicas = jnp.sum(hosting.astype(jnp.int32), axis=1)
    replica = source % replicas
    chosen = (hosting & (replica_rank[None, :] == replica[:, None])).astype(jnp.int32)
    target = jnp.sum(chosen * slot_ids[None, :], axis=1)
    running = jnp.cumsum(chosen.reshape(N_EP, TOK_DEV * TOPK, N_EP), axis=1).reshape(rows_total, N_EP)
    position = jnp.sum((running - 1) * chosen, axis=1)
    table = jnp.full((N_EP, N_EP * CAP), rows_total, jnp.int32)
    table = table.at[target, source * CAP + position].set(jnp.arange(rows_total, dtype=jnp.int32))
    token_rows = jnp.concatenate([jnp.repeat(tokens, TOPK, axis=0), jnp.zeros((1, D), jnp.bfloat16)], axis=0)
    grad_rows = jnp.concatenate([jnp.repeat(out_grad, TOPK, axis=0), jnp.zeros((1, D), jnp.bfloat16)], axis=0)
    prob_rows = jnp.concatenate([route_probs.reshape(-1), jnp.zeros((1,), jnp.bfloat16)], axis=0)
    scaled_rows = (prob_rows.astype(jnp.float32)[:, None] * grad_rows.astype(jnp.float32)).astype(jnp.bfloat16)

    def per_slot(slot):
        index = table[slot]
        inputs = token_rows[index]
        scaled = scaled_rows[index]
        gate_rows = w_gate[slot]
        up_rows = w_up[slot]
        down_rows = w_down[slot]
        gate = split_sum(inputs, gate_rows)
        up_sum = split_sum(inputs, up_rows)
        grad_hidden = split_sum(scaled, down_rows)
        hidden, grad_gate, grad_up = activate(gate, up_sum, grad_hidden)
        part_gate = jnp.dot(inputs.T, grad_gate, preferred_element_type=jnp.float32).astype(jnp.bfloat16)
        part_up = jnp.dot(inputs.T, grad_up, preferred_element_type=jnp.float32).astype(jnp.bfloat16)
        part_down = jnp.dot(scaled.T, hidden, preferred_element_type=jnp.float32).astype(jnp.bfloat16)
        row_grad = (jnp.dot(grad_gate, gate_rows.T, preferred_element_type=jnp.float32)
                    + jnp.dot(grad_up, up_rows.T, preferred_element_type=jnp.float32)).astype(jnp.bfloat16)
        return jnp.stack([part_gate, part_up, part_down]), row_grad

    partials, row_grads = lax.map(per_slot, slot_ids)
    placed = jnp.zeros((rows_total + 1, D), jnp.bfloat16).at[table.reshape(-1)].set(row_grads.reshape(-1, D))
    in_grad = jnp.sum(placed[:rows_total].astype(jnp.float32).reshape(TOKENS, TOPK, D), axis=1).astype(jnp.bfloat16)
    mixed = jnp.dot(same_expert.astype(jnp.bfloat16), partials.reshape(N_EP, -1), preferred_element_type=jnp.float32)
    summed = mixed.astype(jnp.bfloat16).reshape(N_EP, 3, D, H)
    return in_grad, summed[:, 0], summed[:, 1], summed[:, 2]
```

```python
import jax
import jax.numpy as jnp
from jax import lax
from jax.sharding import Mesh, PartitionSpec as P

EP = ("x", "zl", "c")
GRP = ("y", "zh")
BF = jnp.bfloat16
F32 = jnp.float32
CAP = 40


def dot(a, b, dims=((1,), (0,))):
    return lax.dot_general(a, b, (dims, ((), ())), preferred_element_type=F32)


def activate(gate, up_sum, grad_hidden):
    sigma = jax.nn.sigmoid(gate)
    swish = gate * sigma
    hidden = (swish * up_sum).astype(BF)
    grad_up = (grad_hidden * swish).astype(BF)
    grad_gate = (grad_hidden * up_sum * sigma * (1.0 + gate * (1.0 - sigma))).astype(BF)
    return (hidden, grad_gate, grad_up)


def routing(ids, probs, slot_expert):
    count = ids.shape[0]
    slots = slot_expert.shape[0]
    named = ids[:, :, None] == slot_expert[None, None, :]
    sent = jnp.any(named, axis=1)
    weight = jnp.sum(jnp.where(named, probs.astype(F32)[:, :, None], 0.0), axis=1)
    row = lax.broadcasted_iota(jnp.int32, (count, count), 0)
    col = lax.broadcasted_iota(jnp.int32, (count, count), 1)
    pos = dot((row > col).astype(BF), sent.astype(BF)).astype(jnp.int32)
    pos = jnp.where(sent, pos, -1)
    place = lax.broadcasted_iota(jnp.int32, (slots, CAP, count), 1)
    hit = pos.T[:, None, :] == place
    pick = hit.astype(BF).reshape(slots * CAP, count)
    scaled = jnp.where(hit, weight.T[:, None, :], 0.0).astype(BF).reshape(slots * CAP, count)
    slot = jnp.arange(slots)
    same = (slot_expert[:, None] == slot_expert[None, :]) & (slot[:, None] > slot[None, :])
    first = jnp.logical_not(jnp.any(same, axis=1))
    back = (hit & first[:, None, None]).astype(BF).reshape(slots * CAP, count)
    return pick, scaled, back


def swap_half(part):
    half = part.shape[0] // 2
    me = lax.axis_index("zh")
    keep = lax.dynamic_slice_in_dim(part, me * half, half, 0)
    give = lax.dynamic_slice_in_dim(part, (1 - me) * half, half, 0)
    got = lax.ppermute(give, "zh", [(0, 1), (1, 0)])
    return keep.astype(F32) + got.astype(F32)


def join_half(own):
    me = lax.axis_index("zh")
    other = lax.ppermute(own, "zh", [(0, 1), (1, 0)])
    lo = jnp.where(me == 0, own, other)
    hi = jnp.where(me == 0, other, own)
    return jnp.concatenate([lo, hi], axis=0)


def per_device(tokens, out_grad, expert_ids, route_probs, slot_expert, w_gate, w_up, w_down):
    width = tokens.shape[1]
    slots = slot_expert.shape[0]
    rows = slots * CAP
    pick, scaled, back = routing(expert_ids, route_probs, slot_expert)
    send_x = dot(pick, tokens).astype(BF).reshape(slots, CAP, width)
    send_g = dot(scaled, out_grad).astype(BF).reshape(slots, CAP, width)
    xs = lax.all_to_all(send_x, EP, 0, 0, tiled=True).reshape(rows, width)
    gs = lax.all_to_all(send_g, EP, 0, 0, tiled=True).reshape(rows, width)
    wg, wu, wd = w_gate[0], w_up[0], w_down[0]

    def total(part):
        return swap_half(lax.psum_scatter(part.astype(BF), "y", scatter_dimension=0, tiled=True))

    gate = total(dot(xs, wg))
    up = total(dot(xs, wu))
    dh = total(dot(gs, wd))
    hidden, d_gate, d_up = activate(gate, up, dh)

    def whole(own):
        return lax.all_gather(join_half(own), "y", axis=0, tiled=True)

    d_gate, d_up, hidden = whole(d_gate), whole(d_up), whole(hidden)
    rg = (dot(d_gate, wg, ((1,), (1,))) + dot(d_up, wu, ((1,), (1,)))).astype(BF)
    ret = lax.all_to_all(rg.reshape(slots, CAP, width), EP, 0, 0, tiled=True).reshape(rows, width)
    pg = dot(xs, d_gate, ((0,), (0,))).astype(BF)
    pu = dot(xs, d_up, ((0,), (0,))).astype(BF)
    pd = dot(gs, hidden, ((0,), (0,))).astype(BF)
    in_grad = dot(back, ret, ((0,), (0,))).astype(BF)
    return in_grad, pg[None], pu[None], pd[None]


def solution(mesh):
    fine = Mesh(mesh.devices.reshape(4, 2, 4, 4, 2), ("y", "zh", "x", "zl", "c"))
    return jax.shard_map(
        per_device,
        mesh=fine,
        in_specs=(
            P(EP, GRP),
            P(EP, GRP),
            P(EP, None),
            P(EP, None),
            P(),
            P(EP, GRP, None),
            P(EP, GRP, None),
            P(EP, GRP, None),
        ),
        out_specs=(P(EP, GRP), P(EP, GRP, None), P(EP, GRP, None), P(EP, GRP, None)),
        check_vma=False,
    )
```

```python
import jax
import jax.numpy as jnp
from jax import lax
from jax.sharding import Mesh, PartitionSpec as P

EP = ("x", "zl", "c")
GRP = ("y", "zh")
BF = jnp.bfloat16
F32 = jnp.float32
CAP = 40


def dot(a, b, dims=((1,), (0,))):
    return lax.dot_general(a, b, (dims, ((), ())), preferred_element_type=F32)


def activate(gate, up_sum, grad_hidden):
    sigma = jax.nn.sigmoid(gate)
    swish = gate * sigma
    hidden = (swish * up_sum).astype(BF)
    grad_up = (grad_hidden * swish).astype(BF)
    grad_gate = (grad_hidden * up_sum * sigma * (1.0 + gate * (1.0 - sigma))).astype(BF)
    return (hidden, grad_gate, grad_up)


def routing(ids, probs, slot_expert):
    count = ids.shape[0]
    slots = slot_expert.shape[0]
    named = ids[:, :, None] == slot_expert[None, None, :]
    sent = jnp.any(named, axis=1)
    weight = jnp.sum(jnp.where(named, probs.astype(F32)[:, :, None], 0.0), axis=1)
    row = lax.broadcasted_iota(jnp.int32, (count, count), 0)
    col = lax.broadcasted_iota(jnp.int32, (count, count), 1)
    pos = dot((row > col).astype(BF), sent.astype(BF)).astype(jnp.int32)
    pos = jnp.where(sent, pos, -1)
    place = lax.broadcasted_iota(jnp.int32, (slots, CAP, count), 1)
    hit = pos.T[:, None, :] == place
    pick = hit.astype(BF)
    scaled = jnp.where(hit, weight.T[:, None, :], 0.0).astype(BF)
    slot = jnp.arange(slots)
    same = (slot_expert[:, None] == slot_expert[None, :]) & (slot[:, None] > slot[None, :])
    first = jnp.logical_not(jnp.any(same, axis=1))
    back = (hit & first[:, None, None]).astype(BF)
    return pick, scaled, back


def arrange(rows, back):
    y, zh = lax.axis_index("y"), lax.axis_index("zh")
    half = rows.shape[0] // 8
    pieces = []
    for j in range(4):
        for h in range(2):
            quarter = jnp.where(back, j - y, j + y) % 4
            pieces.append(lax.dynamic_slice_in_dim(rows, (2 * quarter + (h + zh) % 2) * half, half, 0))
    return jnp.concatenate(pieces, axis=0)


def turn(value, step):
    return lax.ppermute(value, "y", [(i, (i + step) % 4) for i in range(4)])


def cross(value):
    return lax.ppermute(value, "zh", [(0, 1), (1, 0)])


def ring_sum(part, step):
    block = part.shape[0] // 4

    def own(j):
        j %= 4
        return part[j * block : (j + 1) * block]

    held = own(-step)
    for t in (2, 3, 4):
        held = turn(held, step).astype(F32) + own(-step * t).astype(F32)
        if t < 4:
            held = held.astype(BF)
    return held


def swap_sum(block):
    half = block.shape[0] // 2
    return block[:half] + cross(block[half:].astype(BF)).astype(F32)


def ring_gather(own):
    other = cross(own)
    left0, right0 = turn(own, 1), turn(own, -1)
    left1, right1 = turn(other, 1), turn(other, -1)
    far0, far1 = turn(left0, 1), turn(right1, -1)
    return jnp.concatenate([own, other, right0, right1, far0, far1, left0, left1], axis=0)


SIZES = (24, 16)


def per_device(tokens, out_grad, expert_ids, route_probs, slot_expert, w_gate, w_up, w_down):
    width = tokens.shape[1]
    slots = slot_expert.shape[0]
    count = tokens.shape[0]
    pick, scaled, back = routing(expert_ids, route_probs, slot_expert)
    wg, wu, wd = w_gate[0], w_up[0], w_down[0]

    def dispatch(matrix, values, lo, size):
        part = matrix[:, lo : lo + size].reshape(slots * size, count)
        send = dot(part, values).astype(BF).reshape(slots, size, width)
        got = lax.all_to_all(send, EP, 0, 0, tiled=True).reshape(slots * size, width)
        return arrange(got, False)

    starts = [sum(SIZES[:i]) for i in range(len(SIZES))]
    grads, in_grad = None, None
    for lo, size in zip(starts, SIZES):
        xs = dispatch(pick, tokens, lo, size)
        gate = ring_sum(dot(xs, wg).astype(BF), 1)
        up = ring_sum(dot(xs, wu).astype(BF), -1)
        gs = dispatch(scaled, out_grad, lo, size)
        dh = dot(gs, wd).astype(BF)
        mid = dh.shape[1] // 2
        dh = jnp.concatenate([ring_sum(dh[:, :mid], 1), ring_sum(dh[:, mid:], -1)], axis=1)
        hidden, d_gate, d_up = activate(swap_sum(gate), swap_sum(up), swap_sum(dh))
        d_gate, d_up, hidden = ring_gather(d_gate), ring_gather(d_up), ring_gather(hidden)
        rg = (dot(d_gate, wg, ((1,), (1,))) + dot(d_up, wu, ((1,), (1,)))).astype(BF)
        rg = arrange(rg, True).reshape(slots, size, width)
        ret = lax.all_to_all(rg, EP, 0, 0, tiled=True).reshape(slots * size, width)
        part = back[:, lo : lo + size].reshape(slots * size, count)
        mine = dot(part, ret, ((0,), (0,)))
        in_grad = mine if in_grad is None else in_grad + mine
        new = [dot(xs, d_gate, ((0,), (0,))), dot(xs, d_up, ((0,), (0,))), dot(gs, hidden, ((0,), (0,)))]
        grads = new if grads is None else [p + q for p, q in zip(grads, new)]
    pg, pu, pd = [g.astype(BF) for g in grads]
    return in_grad.astype(BF), pg[None], pu[None], pd[None]


def solution(mesh):
    fine = Mesh(mesh.devices.reshape(4, 2, 4, 4, 2), ("y", "zh", "x", "zl", "c"))
    return jax.shard_map(
        per_device,
        mesh=fine,
        in_specs=(
            P(EP, GRP),
            P(EP, GRP),
            P(EP, None),
            P(EP, None),
            P(),
            P(EP, GRP, None),
            P(EP, GRP, None),
            P(EP, GRP, None),
        ),
        out_specs=(P(EP, GRP), P(EP, GRP, None), P(EP, GRP, None), P(EP, GRP, None)),
        check_vma=False,
    )
```

```python
import jax
import jax.numpy as jnp
from jax import lax
from jax.sharding import Mesh, PartitionSpec as P

EP = ("x", "zl", "c")
GRP = ("y", "zh")
BF = jnp.bfloat16
F32 = jnp.float32
CAP = 40


def dot(a, b, dims=((1,), (0,))):
    return lax.dot_general(a, b, (dims, ((), ())), preferred_element_type=F32)


def activate(gate, up_sum, grad_hidden):
    sigma = jax.nn.sigmoid(gate)
    swish = gate * sigma
    hidden = (swish * up_sum).astype(BF)
    grad_up = (grad_hidden * swish).astype(BF)
    grad_gate = (grad_hidden * up_sum * sigma * (1.0 + gate * (1.0 - sigma))).astype(BF)
    return (hidden, grad_gate, grad_up)


def positions(ids, slots_of):
    count = ids.shape[-2]
    sent = jnp.any(ids[..., None] == slots_of, axis=-2)
    row = lax.broadcasted_iota(jnp.int32, (count, count), 0)
    col = lax.broadcasted_iota(jnp.int32, (count, count), 1)
    below = (row > col).astype(BF)
    pos = jnp.einsum("ut,...ts->...us", below, sent.astype(BF), preferred_element_type=F32)
    return jnp.where(sent, pos.astype(jnp.int32), -1)


def turn(value, step):
    return lax.ppermute(value, "y", [(i, (i + step) % 4) for i in range(4)])


def cross(value):
    return lax.ppermute(value, "zh", [(0, 1), (1, 0)])


def rows_at(value, start, size):
    return lax.dynamic_slice_in_dim(value, start, size, 0)


def after(value, *others):
    return lax.optimization_barrier((value, *others))[0]


def send_y(part):
    y = lax.axis_index("y")
    block = part.shape[0] // 4
    got = [turn(rows_at(part, (y + j) % 4 * block, block), j) for j in (1, 3, 2)]
    return [rows_at(part, y * block, block)] + got


def add_up(pieces):
    total = pieces[0].astype(F32)
    for g in pieces[1:]:
        total = total + g.astype(F32)
    return total


def spread_y(mine):
    half = mine.shape[0] // 2
    left, right = turn(mine, 1), turn(mine, -1)
    far0, far1 = turn(left[:half], 1), turn(right[half:], -1)
    return [mine, left, right, far0, far1]


def lay(pieces):
    y = lax.axis_index("y")
    block, cols = pieces[0].shape
    out = jnp.zeros((4 * block, cols), BF)
    for piece, j, lo in zip(pieces, (0, 3, 1, 2, 2), (0, 0, 0, 0, block // 2)):
        out = lax.dynamic_update_slice(out, piece, ((y + j) % 4 * block + lo, 0))
    return out


SIZES = (24, 16)
WIDE = ("x", "c", "zl")


def per_device(tokens, out_grad, expert_ids, route_probs, slot_expert, w_gate, w_up, w_down):
    count, width = tokens.shape
    slots = slot_expert.shape[0]
    wd = w_down[0]
    wgu = jnp.concatenate([w_gate[0], w_up[0]], axis=1)
    mid = wd.shape[1]
    size0, size1 = SIZES
    mixed = slot_expert.reshape(4, 4, 2).transpose(0, 2, 1).reshape(slots)

    pos = positions(expert_ids, mixed).T

    def picked(where, lo, size):
        place = lax.broadcasted_iota(jnp.int32, (slots, size, count), 1) + lo
        return (where[:, None, :] == place).astype(BF).reshape(slots * size, count)

    def move(value, axes):
        return lax.all_to_all(value, axes, 0, 0, tiled=True)

    def send_x(lo, size):
        return dot(picked(pos, lo, size), tokens).astype(BF).reshape(slots, size, width)

    xs0 = move(send_x(0, size0), WIDE)

    weight = jnp.sum(jnp.where(expert_ids[:, :, None] == mixed, route_probs.astype(F32)[:, :, None], 0.0), axis=1).T

    def send_g(lo, size):
        place = lax.broadcasted_iota(jnp.int32, (slots, size, count), 1) + lo
        matrix = jnp.where(pos[:, None, :] == place, weight[:, None, :], 0.0).astype(BF)
        return dot(matrix.reshape(slots * size, count), out_grad).astype(BF).reshape(slots, size, width)

    gs0 = move(after(send_g(0, size0), xs0), WIDE)
    both1 = jnp.concatenate([send_x(size0, size1), send_g(size0, size1)], axis=2)
    both1 = move(after(both1, gs0), WIDE).reshape(slots * size1, 2 * width)
    xs0, gs0 = xs0.reshape(slots * size0, width), gs0.reshape(slots * size0, width)
    xs1, gs1 = both1[:, :width], both1[:, width:]

    def act(gu, dh):
        hidden, d_gate, d_up = activate(gu[:, :mid], gu[:, mid:], dh)
        return jnp.concatenate([d_gate, d_up, hidden], axis=1)

    gu0 = send_y(dot(xs0, wgu).astype(BF))
    dh0 = send_y(dot(gs0, wd).astype(BF))
    gu0[0] = after(gu0[0], xs1, gs1, dh0[1])
    gu0_sum = add_up(gu0)
    gu0_got = cross(gu0_sum.astype(BF))
    dh0_sum = add_up(dh0)
    dh0_got = cross(dh0_sum.astype(BF))
    part1 = jnp.concatenate([dot(xs1, wgu).astype(BF), dot(gs1, wd).astype(BF)], axis=1)
    part1 = after(part1, *gu0, *dh0)
    all1 = send_y(part1)
    own0 = act(gu0_sum + gu0_got.astype(F32), dh0_sum + dh0_got.astype(F32))
    all1[0] = after(all1[0], gu0_got, dh0_got)
    own0 = after(own0, *all1)
    all1_sum = add_up(all1)
    all1_got = cross(all1_sum.astype(BF))
    got0 = spread_y(own0)
    all1_got = after(all1_got, got0[1], got0[2])
    all1_sum = all1_sum + all1_got.astype(F32)
    own1 = act(all1_sum[:, : 2 * mid], all1_sum[:, 2 * mid :])
    own1 = after(own1, got0[3], got0[4])
    got1 = spread_y(own1)

    slot = jnp.arange(slots)
    same = (mixed[:, None] == mixed[None, :]) & (slot[:, None] > slot[None, :])
    first = jnp.logical_not(jnp.any(same, axis=1))
    where_to = jnp.where(first[:, None], pos, -1)

    def back(ret, lo, size):
        return dot(picked(where_to, lo, size), ret.reshape(slots * size, width), ((0,), (0,)))

    def row_grad(full, size):
        rg = dot(full[:, : 2 * mid], wgu, ((1,), (1,))).astype(BF)
        return move(rg.reshape(slots, size, width), WIDE)

    def weight_grad(full, xs, gs):
        return [
            dot(xs, full[:, :mid], ((0,), (0,))),
            dot(xs, full[:, mid : 2 * mid], ((0,), (0,))),
            dot(gs, full[:, 2 * mid :], ((0,), (0,))),
        ]

    full0 = lay(got0)
    ret0 = row_grad(full0, size0)
    full0 = after(full0, got1[1], got1[2])
    parts0 = weight_grad(full0, xs0, gs0)
    got1[3] = after(got1[3], *parts0)
    full1 = lay(got1)
    ret1 = row_grad(full1, size1)
    gs1 = after(gs1, ret1)
    parts1 = weight_grad(full1, xs1, gs1)
    in_grad = (back(ret0, 0, size0) + back(ret1, size0, size1)).astype(BF)
    pg, pu, pd = [(p + q).astype(BF) for p, q in zip(parts0, parts1)]
    return in_grad, pg[None], pu[None], pd[None]


def solution(mesh):
    fine = Mesh(mesh.devices.reshape(4, 2, 4, 4, 2), ("y", "zh", "x", "zl", "c"))
    return jax.shard_map(
        per_device,
        mesh=fine,
        in_specs=(
            P(EP, GRP),
            P(EP, GRP),
            P(EP, None),
            P(EP, None),
            P(),
            P(EP, GRP, None),
            P(EP, GRP, None),
            P(EP, GRP, None),
        ),
        out_specs=(P(EP, GRP), P(EP, GRP, None), P(EP, GRP, None), P(EP, GRP, None)),
        check_vma=False,
    )
```

```python
import jax
import jax.numpy as jnp
from jax import lax
from jax.sharding import Mesh, PartitionSpec as P

EP = ("x", "zl", "c")
GRP = ("y", "zh")
BF = jnp.bfloat16
F32 = jnp.float32
CAP = 40


def dot(a, b, dims=((1,), (0,))):
    return lax.dot_general(a, b, (dims, ((), ())), preferred_element_type=F32)


def activate(gate, up_sum, grad_hidden):
    sigma = jax.nn.sigmoid(gate)
    swish = gate * sigma
    hidden = (swish * up_sum).astype(BF)
    grad_up = (grad_hidden * swish).astype(BF)
    grad_gate = (grad_hidden * up_sum * sigma * (1.0 + gate * (1.0 - sigma))).astype(BF)
    return (hidden, grad_gate, grad_up)


def positions(ids, slots_of):
    count = ids.shape[-2]
    sent = jnp.any(ids[..., None] == slots_of, axis=-2)
    row = lax.broadcasted_iota(jnp.int32, (count, count), 0)
    col = lax.broadcasted_iota(jnp.int32, (count, count), 1)
    below = (row > col).astype(BF)
    pos = jnp.einsum("ut,...ts->...us", below, sent.astype(BF), preferred_element_type=F32)
    return jnp.where(sent, pos.astype(jnp.int32), -1)


def turn(value, step):
    return lax.ppermute(value, "y", [(i, (i + step) % 4) for i in range(4)])


def cross(value):
    return lax.ppermute(value, "zh", [(0, 1), (1, 0)])


def rows_at(value, start, size):
    return lax.dynamic_slice_in_dim(value, start, size, 0)


def after(value, *others):
    return lax.optimization_barrier((value, *others))[0]


def send_y(part):
    y = lax.axis_index("y")
    block = part.shape[0] // 4
    got = [turn(rows_at(part, (y + j) % 4 * block, block), j) for j in (1, 3, 2)]
    return [rows_at(part, y * block, block)] + got


def sum_y(part):
    return [lax.psum_scatter(part, "y", scatter_dimension=0, tiled=True)]


def add_up(pieces):
    total = pieces[0].astype(F32)
    for g in pieces[1:]:
        total = total + g.astype(F32)
    return total


def spread_y(mine):
    half = mine.shape[0] // 2
    left, right = turn(mine, 1), turn(mine, -1)
    far0, far1 = turn(left[:half], 1), turn(right[half:], -1)
    return [mine, left, right, far0, far1]


def lay(pieces):
    y = lax.axis_index("y")
    block, cols = pieces[0].shape
    out = jnp.zeros((4 * block, cols), BF)
    for piece, j, lo in zip(pieces, (0, 3, 1, 2, 2), (0, 0, 0, 0, block // 2)):
        out = lax.dynamic_update_slice(out, piece, ((y + j) % 4 * block + lo, 0))
    return out


SIZES = (24, 16)
WIDE = ("x", "c", "zl")


def per_device(tokens, out_grad, expert_ids, route_probs, slot_expert, w_gate, w_up, w_down):
    count, width = tokens.shape
    slots = slot_expert.shape[0]
    wd = w_down[0]
    wgu = jnp.concatenate([w_gate[0], w_up[0]], axis=1)
    mid = wd.shape[1]
    size0, size1 = SIZES
    mixed = slot_expert.reshape(4, 4, 2).transpose(0, 2, 1).reshape(slots)

    pos = positions(expert_ids, mixed).T

    def picked(where, lo, size):
        place = lax.broadcasted_iota(jnp.int32, (slots, size, count), 1) + lo
        return (where[:, None, :] == place).astype(BF).reshape(slots * size, count)

    def move(value, axes):
        return lax.all_to_all(value, axes, 0, 0, tiled=True)

    def send_x(lo, size):
        return dot(picked(pos, lo, size), tokens).astype(BF).reshape(slots, size, width)

    xs0 = move(send_x(0, size0), WIDE)

    weight = jnp.sum(jnp.where(expert_ids[:, :, None] == mixed, route_probs.astype(F32)[:, :, None], 0.0), axis=1).T

    def send_g(lo, size):
        place = lax.broadcasted_iota(jnp.int32, (slots, size, count), 1) + lo
        matrix = jnp.where(pos[:, None, :] == place, weight[:, None, :], 0.0).astype(BF)
        return dot(matrix.reshape(slots * size, count), out_grad).astype(BF).reshape(slots, size, width)

    gs0 = move(after(send_g(0, size0), xs0), WIDE)
    both1 = jnp.concatenate([send_x(size0, size1), send_g(size0, size1)], axis=2)
    both1 = move(after(both1, gs0), WIDE).reshape(slots * size1, 2 * width)
    xs0, gs0 = xs0.reshape(slots * size0, width), gs0.reshape(slots * size0, width)
    xs1, gs1 = both1[:, :width], both1[:, width:]

    def act(gu, dh):
        hidden, d_gate, d_up = activate(gu[:, :mid], gu[:, mid:], dh)
        return jnp.concatenate([d_gate, d_up, hidden], axis=1)

    gu0 = sum_y(dot(xs0, wgu).astype(BF))
    dh0 = send_y(dot(gs0, wd).astype(BF))
    gu0_sum = add_up(gu0)
    gu0_got = cross(gu0_sum.astype(BF))
    dh0_sum = add_up(dh0)
    dh0_got = cross(dh0_sum.astype(BF))
    part1 = jnp.concatenate([dot(xs1, wgu).astype(BF), dot(gs1, wd).astype(BF)], axis=1)
    part1 = after(part1, *dh0)
    all1 = send_y(part1)
    own0 = act(gu0_sum + gu0_got.astype(F32), dh0_sum + dh0_got.astype(F32))
    all1[0] = after(all1[0], gu0_got, dh0_got)
    own0 = after(own0, *all1)
    all1_sum = add_up(all1)
    all1_got = cross(all1_sum.astype(BF))
    got0 = spread_y(own0)
    all1_got = after(all1_got, got0[1], got0[2])
    all1_sum = all1_sum + all1_got.astype(F32)
    own1 = act(all1_sum[:, : 2 * mid], all1_sum[:, 2 * mid :])
    own1 = after(own1, got0[3], got0[4])
    got1 = spread_y(own1)

    slot = jnp.arange(slots)
    same = (mixed[:, None] == mixed[None, :]) & (slot[:, None] > slot[None, :])
    first = jnp.logical_not(jnp.any(same, axis=1))
    where_to = jnp.where(first[:, None], pos, -1)

    def back(ret, lo, size):
        return dot(picked(where_to, lo, size), ret.reshape(slots * size, width), ((0,), (0,)))

    def row_grad(full, size):
        rg = dot(full[:, : 2 * mid], wgu, ((1,), (1,))).astype(BF)
        return move(rg.reshape(slots, size, width), WIDE)

    def weight_grad(full, xs, gs):
        return [
            dot(xs, full[:, :mid], ((0,), (0,))),
            dot(xs, full[:, mid : 2 * mid], ((0,), (0,))),
            dot(gs, full[:, 2 * mid :], ((0,), (0,))),
        ]

    full0 = lay(got0)
    ret0 = row_grad(full0, size0)
    full0 = after(full0, got1[1], got1[2])
    parts0 = weight_grad(full0, xs0, gs0)
    got1[3] = after(got1[3], *parts0)
    full1 = lay(got1)
    ret1 = row_grad(full1, size1)
    parts1 = weight_grad(full1, xs1, gs1)
    in_grad = (back(ret0, 0, size0) + back(ret1, size0, size1)).astype(BF)
    pg, pu, pd = [(p + q).astype(BF) for p, q in zip(parts0, parts1)]
    return in_grad, pg[None], pu[None], pd[None]


def solution(mesh):
    fine = Mesh(mesh.devices.reshape(4, 2, 4, 4, 2), ("y", "zh", "x", "zl", "c"))
    return jax.shard_map(
        per_device,
        mesh=fine,
        in_specs=(
            P(EP, GRP),
            P(EP, GRP),
            P(EP, None),
            P(EP, None),
            P(),
            P(EP, GRP, None),
            P(EP, GRP, None),
            P(EP, GRP, None),
        ),
        out_specs=(P(EP, GRP), P(EP, GRP, None), P(EP, GRP, None), P(EP, GRP, None)),
        check_vma=False,
    )
```

```python
import jax
import jax.numpy as jnp
from jax import lax
from jax.sharding import Mesh, PartitionSpec as P

EP = ("x", "zl", "c")
GRP = ("y", "zh")
BF = jnp.bfloat16
F32 = jnp.float32
CAP = 40


def dot(a, b, dims=((1,), (0,))):
    return lax.dot_general(a, b, (dims, ((), ())), preferred_element_type=F32)


def activate(gate, up_sum, grad_hidden):
    sigma = jax.nn.sigmoid(gate)
    swish = gate * sigma
    hidden = (swish * up_sum).astype(BF)
    grad_up = (grad_hidden * swish).astype(BF)
    grad_gate = (grad_hidden * up_sum * sigma * (1.0 + gate * (1.0 - sigma))).astype(BF)
    return (hidden, grad_gate, grad_up)


def positions(ids, slots_of):
    count = ids.shape[-2]
    sent = jnp.any(ids[..., None] == slots_of, axis=-2)
    row = lax.broadcasted_iota(jnp.int32, (count, count), 0)
    col = lax.broadcasted_iota(jnp.int32, (count, count), 1)
    below = (row > col).astype(BF)
    pos = jnp.einsum("ut,...ts->...us", below, sent.astype(BF), preferred_element_type=F32)
    return jnp.where(sent, pos.astype(jnp.int32), -1)


def turn(value, step):
    return lax.ppermute(value, "y", [(i, (i + step) % 4) for i in range(4)])


def cross(value):
    return lax.ppermute(value, "zh", [(0, 1), (1, 0)])


def rows_at(value, start, size):
    return lax.dynamic_slice_in_dim(value, start, size, 0)


def after(value, *others):
    return lax.optimization_barrier((value, *others))[0]


def send_y(part):
    y = lax.axis_index("y")
    block = part.shape[0] // 4
    got = [turn(rows_at(part, (y + j) % 4 * block, block), j) for j in (1, 3, 2)]
    return [rows_at(part, y * block, block)] + got


def sum_y(part):
    return [lax.psum_scatter(part, "y", scatter_dimension=0, tiled=True)]


def add_up(pieces):
    total = pieces[0].astype(F32)
    for g in pieces[1:]:
        total = total + g.astype(F32)
    return total


def spread_y(mine):
    half = mine.shape[0] // 2
    left, right = turn(mine, 1), turn(mine, -1)
    far0, far1 = turn(left[:half], 1), turn(right[half:], -1)
    return [mine, left, right, far0, far1]


def lay(pieces):
    y = lax.axis_index("y")
    block, cols = pieces[0].shape
    out = jnp.zeros((4 * block, cols), BF)
    for piece, j, lo in zip(pieces, (0, 3, 1, 2, 2), (0, 0, 0, 0, block // 2)):
        out = lax.dynamic_update_slice(out, piece, ((y + j) % 4 * block + lo, 0))
    return out


SIZES = (24, 16)
WIDE = ("x", "c", "zl")


def per_device(tokens, out_grad, expert_ids, route_probs, slot_expert, w_gate, w_up, w_down):
    count, width = tokens.shape
    slots = slot_expert.shape[0]
    wd = w_down[0]
    wgu = jnp.concatenate([w_gate[0], w_up[0]], axis=1)
    mid = wd.shape[1]
    size0, size1 = SIZES
    mixed = slot_expert.reshape(4, 4, 2).transpose(0, 2, 1).reshape(slots)

    pos = positions(expert_ids, mixed).T

    def picked(where, lo, size):
        place = lax.broadcasted_iota(jnp.int32, (slots, size, count), 1) + lo
        return (where[:, None, :] == place).astype(BF).reshape(slots * size, count)

    def move(value, axes):
        return lax.all_to_all(value, axes, 0, 0, tiled=True)

    def send_x(lo, size):
        return dot(picked(pos, lo, size), tokens).astype(BF).reshape(slots, size, width)

    xs0 = move(send_x(0, size0), WIDE)

    weight = jnp.sum(jnp.where(expert_ids[:, :, None] == mixed, route_probs.astype(F32)[:, :, None], 0.0), axis=1).T

    def send_g(lo, size):
        place = lax.broadcasted_iota(jnp.int32, (slots, size, count), 1) + lo
        matrix = jnp.where(pos[:, None, :] == place, weight[:, None, :], 0.0).astype(BF)
        return dot(matrix.reshape(slots * size, count), out_grad).astype(BF).reshape(slots, size, width)

    gs0 = move(after(send_g(0, size0), xs0), WIDE)
    both1 = jnp.concatenate([send_x(size0, size1), send_g(size0, size1)], axis=2)
    both1 = move(after(both1, gs0), WIDE).reshape(slots * size1, 2 * width)
    xs0, gs0 = xs0.reshape(slots * size0, width), gs0.reshape(slots * size0, width)
    xs1, gs1 = both1[:, :width], both1[:, width:]

    def act(gu, dh):
        hidden, d_gate, d_up = activate(gu[:, :mid], gu[:, mid:], dh)
        return jnp.concatenate([d_gate, d_up, hidden], axis=1)

    gu0 = sum_y(dot(xs0, wgu).astype(BF))
    dh0 = send_y(dot(gs0, wd).astype(BF))
    gu0_sum = add_up(gu0)
    gu0_got = cross(gu0_sum.astype(BF))
    dh0_sum = add_up(dh0)
    dh0_got = cross(dh0_sum.astype(BF))
    part1 = jnp.concatenate([dot(xs1, wgu).astype(BF), dot(gs1, wd).astype(BF)], axis=1)
    part1 = after(part1, *dh0)
    all1 = send_y(part1)
    own0 = act(gu0_sum + gu0_got.astype(F32), dh0_sum + dh0_got.astype(F32))
    all1[0] = after(all1[0], gu0_got, dh0_got)
    own0 = after(own0, *all1)
    all1_sum = add_up(all1)
    all1_got = cross(all1_sum.astype(BF))
    got0 = spread_y(own0)
    all1_got = after(all1_got, got0[1], got0[2])
    all1_sum = all1_sum + all1_got.astype(F32)
    own1 = act(all1_sum[:, : 2 * mid], all1_sum[:, 2 * mid :])
    own1 = after(own1, got0[3], got0[4])
    got1 = spread_y(own1)

    slot = jnp.arange(slots)
    same = (mixed[:, None] == mixed[None, :]) & (slot[:, None] > slot[None, :])
    first = jnp.logical_not(jnp.any(same, axis=1))
    where_to = jnp.where(first[:, None], pos, -1)

    def back(ret, lo, size):
        return dot(picked(where_to, lo, size), ret.reshape(slots * size, width), ((0,), (0,)))

    def row_grad(full, size):
        rg = dot(full[:, : 2 * mid], wgu, ((1,), (1,))).astype(BF)
        return move(rg.reshape(slots, size, width), WIDE)

    def weight_grad(full, xs, gs):
        return [
            dot(xs, full[:, :mid], ((0,), (0,))),
            dot(xs, full[:, mid : 2 * mid], ((0,), (0,))),
            dot(gs, full[:, 2 * mid :], ((0,), (0,))),
        ]

    full0 = lay(got0)
    ret0 = row_grad(full0, size0)
    full0 = after(full0, got1[1], got1[2])
    parts0 = weight_grad(full0, xs0, gs0)
    got1[3] = after(got1[3], *parts0[:2])
    full1 = lay(got1)
    ret1 = row_grad(full1, size1)
    parts1 = weight_grad(full1, xs1, gs1)
    in_grad = (back(ret0, 0, size0) + back(ret1, size0, size1)).astype(BF)
    pg, pu, pd = [(p + q).astype(BF) for p, q in zip(parts0, parts1)]
    return in_grad, pg[None], pu[None], pd[None]


def solution(mesh):
    fine = Mesh(mesh.devices.reshape(4, 2, 4, 4, 2), ("y", "zh", "x", "zl", "c"))
    return jax.shard_map(
        per_device,
        mesh=fine,
        in_specs=(
            P(EP, GRP),
            P(EP, GRP),
            P(EP, None),
            P(EP, None),
            P(),
            P(EP, GRP, None),
            P(EP, GRP, None),
            P(EP, GRP, None),
        ),
        out_specs=(P(EP, GRP), P(EP, GRP, None), P(EP, GRP, None), P(EP, GRP, None)),
        check_vma=False,
    )
```
